32 devices in a mesh: cuts: 2 (over core), tile: 16 (over z, y, x).
Axes of the slice: x: 2, y: 2, z: 4, core: 2. Of those that a mesh axis runs over, the one named last changes fastest.
Arguments:
- transmission: float32 [2, 2, 4096, 512], P(None, 'cuts', 'tile')
- illumination: float32 [2, 256, 256], replicated, may hold values from -6 to 6
- measured: float32 [16, 256, 256], P('tile'), may hold values from 0.2 to 5
- offsets: int32 [16, 2], P('tile'), may hold values from 0 to 256, as said below
- live_count: int32 [16], P('tile'), may hold values from 1 to 1, as said below
Outputs:
- object_grad: float32 [2, 2, 4096, 512], P(None, 'cuts', 'tile')
The draws below stay inside these ranges and needn't reach their ends.
Inputs may be any that keep to these rules, and one draw needn't show every extreme that they name: offsets[j, 0] counts rows from the first row of tile j // 1 and may run past that tile's end (past the last tile, into the first); offsets[j, 1] counts columns; in every draw some live slot has row 255 and column 256. `live_count`: slots of a tile at or beyond its count are unused; some tile has all 1 slots used in every draw.
All inputs are finite; a program needn't handle non-finite values.
Results may differ from the reference program's by a relative error of at most 0.0049.
Values may be sent and summed in bfloat16 or wider, within the bound.
A program may use at most 64 MiB of HBM per device.

```python
import math
import jax
import jax.numpy as jnp
from jax import lax

PW = 256
S_DEV = 1
TY = 256
WX = 512
P_DEV = 1
SLICES = 2
NY = 4096
PROBES = 16
N_TILE = 16


def draw_transmission(key, part):
    key_amp, key_phase = jax.random.split(jax.random.fold_in(key, 11))
    shape = (SLICES, NY, WX)
    amplitude = 1.0 + 0.1 * jax.random.normal(key_amp, shape, jnp.float32)
    phase = 0.35 * jax.random.normal(key_phase, shape, jnp.float32)
    return jnp.stack([amplitude * jnp.cos(phase), amplitude * jnp.sin(phase)], axis=0).astype(jnp.float32)


def draw_offsets(key, part):
    keys = jax.random.split(jax.random.fold_in(key, 23), 4)
    row_values = jax.random.randint(keys[0], (PROBES,), 0, TY)
    col_values = jax.random.randint(keys[1], (PROBES,), 0, WX - PW + 1)
    high_tile = jax.random.randint(keys[2], (), 0, N_TILE)
    low_tile = (high_tile + 1 + jax.random.randint(keys[3], (), 0, max(N_TILE - 1, 1))) % N_TILE
    row_values = row_values.at[high_tile * P_DEV].set(TY - 1).at[low_tile * P_DEV].set(0)
    col_values = col_values.at[high_tile * P_DEV].set(WX - PW).at[low_tile * P_DEV].set(0)
    return jnp.stack([row_values, col_values], axis=1).astype(jnp.int32)


def draw_live_count(key, part):
    keys = jax.random.split(jax.random.fold_in(key, 37), 2)
    counts = jax.random.randint(keys[0], (N_TILE,), 1, P_DEV + 1)
    full_tile = jax.random.randint(keys[1], (), 0, N_TILE)
    return counts.at[full_tile].set(P_DEV).astype(jnp.int32)


def shard_levels(rng, extent, cuts, smallest, high):
    def one(dim, parts):
        steps = jax.random.uniform(jax.random.fold_in(jax.random.fold_in(rng, 6), dim), (parts,), jnp.float32, smallest / len(cuts), high / len(cuts))
        return jnp.repeat(jnp.exp(steps), extent[dim] // parts).reshape((-1,) + (1,) * (len(extent) - dim - 1))

    level = one(*cuts[0])
    for cut in cuts[1:]:
        level = level * one(*cut)
    return level


def gaussian(rng, dims, scale, reach, held_as=jnp.bfloat16):
    entries = jax.random.normal(rng, dims, jnp.float32) * scale
    return jnp.minimum(jnp.maximum(entries, -reach), reach).astype(held_as)


def setup_inputs(seed: int = 0) -> dict:
    streams_of = jax.random.split(jax.random.key(seed), 6)
    return {
        "transmission": draw_transmission(jax.random.fold_in(streams_of[5], 71), 0),
        "illumination": gaussian(streams_of[1], (2, PW, PW), 0.7, 6.0, jnp.float32),
        "measured": jnp.clip(jnp.exp(math.log(5.0) - 3.218876 * jax.random.uniform(streams_of[2], (PROBES, PW, PW), jnp.float32) ** shard_levels(streams_of[2], (PROBES, PW, PW), ((0, 16),), -0.2, 0.2)), 0.2, 5.0),
        "offsets": draw_offsets(jax.random.fold_in(streams_of[5], 71), 0),
        "live_count": draw_live_count(jax.random.fold_in(streams_of[5], 71), 0),
    }


def fresnel_tables(patch_width):
    freq = jnp.arange(patch_width, dtype=jnp.int32)
    signed = jnp.where(freq < patch_width // 2, freq, freq - patch_width).astype(jnp.float32)
    phases = math.pi * signed * signed / (4.0 * patch_width)
    product = freq[:, None] * freq[None, :] % patch_width
    angles = 2.0 * math.pi * product.astype(jnp.float32) / patch_width
    cos_table = jnp.cos(angles)
    sin_table = jnp.sin(angles)
    shifted_real = jnp.cos(angles - phases[None, :])
    shifted_imag = jnp.sin(angles - phases[None, :])
    highest = lax.Precision.HIGHEST
    prop_real = (jnp.dot(shifted_real, cos_table, precision=highest) + jnp.dot(shifted_imag, sin_table, precision=highest)) / patch_width
    prop_imag = (jnp.dot(shifted_imag, cos_table, precision=highest) - jnp.dot(shifted_real, sin_table, precision=highest)) / patch_width
    factor = 1.0 / math.sqrt(patch_width)
    far_real = cos_table * factor
    far_imag = -sin_table * factor
    return (prop_real, prop_imag, far_real, far_imag)

def left_product(mat_real, mat_imag, real_part, imag_part):
    width = mat_real.shape[0]
    stacked = jnp.concatenate([jnp.concatenate([mat_real, -mat_imag], axis=1), jnp.concatenate([mat_imag, mat_real], axis=1)], axis=0)
    values = jnp.concatenate([real_part, imag_part], axis=-2)
    result = jnp.einsum('ab,...bc->...ac', stacked, values, precision=lax.Precision.HIGHEST)
    return (result[..., :width, :], result[..., width:, :])

def right_product(real_part, imag_part, mat_real, mat_imag):
    width = mat_real.shape[1]
    stacked = jnp.concatenate([jnp.concatenate([mat_real, mat_imag], axis=1), jnp.concatenate([-mat_imag, mat_real], axis=1)], axis=0)
    values = jnp.concatenate([real_part, imag_part], axis=-1)
    result = jnp.einsum('...ab,bc->...ac', values, stacked, precision=lax.Precision.HIGHEST)
    return (result[..., :width], result[..., width:])

def apply_forward(mat_real, mat_imag, real_part, imag_part):
    left_real, left_imag = left_product(mat_real, mat_imag, real_part, imag_part)
    return right_product(left_real, left_imag, mat_real.T, mat_imag.T)

def apply_adjoint(mat_real, mat_imag, real_part, imag_part):
    left_real, left_imag = left_product(mat_real.T, -mat_imag.T, real_part, imag_part)
    return right_product(left_real, left_imag, mat_real, -mat_imag)

def complex_times(first_real, first_imag, second_real, second_imag):
    return (first_real * second_real - first_imag * second_imag, first_real * second_imag + first_imag * second_real)

def conj_times(first_real, first_imag, second_real, second_imag):
    return (first_real * second_real + first_imag * second_imag, first_real * second_imag - first_imag * second_real)

def to_half(values):
    rounded = lax.optimization_barrier(values.astype(jnp.bfloat16))
    return rounded.astype(jnp.float32)

def one_probe(patch, illumination, target, flag, tables):
    prop_real, prop_imag, far_real, far_imag = tables
    wave_real = illumination[0]
    wave_imag = illumination[1]
    saved_waves = []
    for layer_index in range(SLICES):
        if layer_index > 0 and layer_index % S_DEV == 0:
            wave_real = to_half(wave_real)
            wave_imag = to_half(wave_imag)
        saved_waves.append((wave_real, wave_imag))
        chi_real, chi_imag = complex_times(wave_real, wave_imag, patch[0, layer_index], patch[1, layer_index])
        wave_real, wave_imag = apply_forward(prop_real, prop_imag, chi_real, chi_imag)
    out_real, out_imag = apply_forward(far_real, far_imag, wave_real, wave_imag)
    weight = (out_real * out_real + out_imag * out_imag - target) * flag
    grad_real, grad_imag = apply_adjoint(far_real, far_imag, weight * out_real, weight * out_imag)
    pieces = [None] * SLICES
    for layer_index in reversed(range(SLICES)):
        chi_real, chi_imag = apply_adjoint(prop_real, prop_imag, grad_real, grad_imag)
        kept_real, kept_imag = saved_waves[layer_index]
        pieces[layer_index] = jnp.stack(conj_times(kept_real, kept_imag, chi_real, chi_imag), axis=0)
        grad_real, grad_imag = conj_times(patch[0, layer_index], patch[1, layer_index], chi_real, chi_imag)
        if layer_index > 0 and layer_index % S_DEV == 0:
            grad_real = to_half(grad_real)
            grad_imag = to_half(grad_imag)
    return jnp.stack(pieces, axis=1)

def reference(transmission, illumination, measured, offsets, live_count):
    tables = fresnel_tables(PW)
    extended = jnp.concatenate([transmission, transmission[:, :, :PW, :]], axis=2)
    slot_index = jnp.arange(PROBES, dtype=jnp.int32)
    owner = slot_index // P_DEV
    live_flags = (slot_index % P_DEV < live_count[owner]).astype(jnp.float32)
    row_starts = (owner * TY + offsets[:, 0]).astype(jnp.int32)
    col_starts = offsets[:, 1].astype(jnp.int32)
    anchor = jnp.zeros((), jnp.int32)

    def add_probe(total, item):
        row_start, col_start, target, flag = item
        corner = (anchor, anchor, row_start, col_start)
        patch = lax.dynamic_slice(extended, corner, (2, SLICES, PW, PW))
        piece = one_probe(patch, illumination, target, flag, tables)
        current = lax.dynamic_slice(total, corner, (2, SLICES, PW, PW))
        return (lax.dynamic_update_slice(total, current + piece, corner), None)
    total, _ = lax.scan(add_probe, jnp.zeros_like(extended), (row_starts, col_starts, measured, live_flags))
    return total[:, :, :NY].at[:, :, :PW].add(total[:, :, NY:])
```

```python
import functools
import math

import jax
import jax.numpy as jnp
import ml_dtypes
import numpy as np
from jax import lax
from jax.experimental import pallas as pl
from jax.experimental.pallas import tpu as pltpu
from jax.sharding import PartitionSpec as P

MESH = pl.DeviceIdType.MESH
F32 = jnp.float32
BF16 = jnp.bfloat16


def split_pair(value):
    high = value.astype(ml_dtypes.bfloat16)
    low = (value - high.astype(np.float64)).astype(ml_dtypes.bfloat16)
    return high, low


def constant_tables(width):
    freq = np.arange(width)
    signed = np.where(freq < width // 2, freq, freq - width).astype(np.float64)
    phases = math.pi * signed * signed / (4.0 * width)
    waves = np.exp(2j * math.pi * (freq[:, None] * freq[None, :] % width) / width)
    prop = (waves * np.exp(-1j * phases)[None, :]) @ waves.conj().T / width
    far = waves.conj() / math.sqrt(width)
    rows = []
    for mat in (prop, far):
        right = np.block([[mat.real, mat.imag], [-mat.imag, mat.real]])
        left = np.block([[mat.real, -mat.imag], [mat.imag, mat.real]])
        rows.append(np.stack(split_pair(right) + split_pair(left)))
    return np.stack(rows)


def halves(value):
    high = value.astype(BF16)
    low = (value - high.astype(F32)).astype(BF16)
    return high, low


def dot(a, b):
    return jnp.dot(a, b, preferred_element_type=F32)


def from_right(value, mats, at):
    high, low = halves(value)
    return dot(high, mats[at]) + (dot(low, mats[at]) + dot(high, mats[at + 1]))


def from_left(value, mats, at):
    high, low = halves(value)
    return dot(mats[at], high) + (dot(mats[at], low) + dot(mats[at + 1], high))


def beside(stacked):
    width = stacked.shape[0] // 2
    return jnp.concatenate([stacked[:width], stacked[width:]], axis=1)


def above(flat):
    width = flat.shape[1] // 2
    return jnp.concatenate([flat[:, :width], flat[:, width:]], axis=0)


def times(ar, ai, br, bi):
    return ar * br - ai * bi, ar * bi + ai * br


def conj_times(ar, ai, br, bi):
    return ar * br + ai * bi, ar * bi - ai * br


def one_hot(shape, along, offset, start=0):
    ahead = lax.broadcasted_iota(jnp.int32, shape, along) + start
    gap = ahead - lax.broadcasted_iota(jnp.int32, shape, 1 - along)
    return jnp.where(gap == offset, 1.0, 0.0).astype(BF16)


def moved_right(value, mask):
    high, low = halves(value)
    return dot(high, mask) + dot(low, mask)


def moved_left(mask, value):
    high, low = halves(value)
    return dot(mask, high) + dot(mask, low)


def kernel(
    tiles,
    trans_hbm,
    illum_hbm,
    measured_hbm,
    offs_hbm,
    live_hbm,
    tables,
    out,
    trans,
    illum,
    measured,
    offs,
    live,
    mats,
    off_out,
    off_in,
    code_out,
    code_in,
    level_out,
    level_in,
    wave,
    back,
    wave_out,
    back_out,
    grads,
    spill_out,
    spill_in,
    local_sem,
    send_sem,
    recv_sem,
):
    cut = lax.axis_index("cuts")
    tile = lax.axis_index("tile")
    before = lax.rem(tile + tiles - 1, tiles)
    after = lax.rem(tile + 1, tiles)
    other = 1 - cut
    rows, cols = trans.shape[1], trans.shape[2]
    width = illum.shape[1]

    barrier = pltpu.get_barrier_semaphore()
    for target in ((cut, before), (cut, after), (other, tile)):
        pl.semaphore_signal(barrier, inc=1, device_id=target, device_id_type=MESH)
    local = []
    for source, target in (
        (offs_hbm, offs),
        (live_hbm, live),
        (trans_hbm, trans),
        (illum_hbm, illum),
        (measured_hbm, measured),
        (tables.at[cut], mats),
    ):
        copy = pltpu.make_async_copy(source, target, local_sem.at[len(local)])
        copy.start()
        local.append(copy)
    local[0].wait()
    row_at = offs[0:1, 0:1]
    col_at = offs[0:1, 1:2]
    off_out[...] = jnp.broadcast_to(col_at, off_out.shape)
    pl.semaphore_wait(barrier, 3)

    def remote(src, dst, at, target):
        return pltpu.make_async_remote_copy(
            src_ref=src,
            dst_ref=dst,
            send_sem=send_sem.at[at],
            recv_sem=recv_sem.at[at],
            device_id=target,
            device_id_type=MESH,
        )

    off_copy = remote(off_out, off_in, 0, (cut, after))
    off_copy.start()
    for copy in local[1:]:
        copy.wait()
    flag = jnp.where(live[0:1, 0:1] > 0, 1.0, 0.0)
    own = jnp.concatenate([trans[0], trans[1]], axis=0)
    high, low = halves(own)
    off_copy.wait()
    next_at = off_in[0:1, 0:1]
    pick = one_hot((cols, width), 0, next_at)
    picked = dot(high, pick) + dot(low, pick)
    level = jnp.maximum(jnp.max(jnp.abs(picked), axis=0, keepdims=True), 1e-30) * (1.0 / 32767.0)
    level_out[...] = jnp.broadcast_to(level, level_out.shape)
    level_copy = remote(level_out, level_in, 1, (cut, before))
    level_copy.start()
    code_out[...] = jnp.round(picked / level).astype(jnp.int32).astype(jnp.int16)
    code_copy = remote(code_out, code_in, 2, (cut, before))
    code_copy.start()

    pick = one_hot((cols, width), 0, col_at)
    mine = beside(dot(high, pick) + dot(low, pick))
    mine = moved_left(one_hot((width, rows), 1, row_at), mine)
    row_pick = one_hot((width, rows), 1, row_at, rows)
    level_copy.wait()
    code_copy.wait()
    theirs = code_in[...].astype(jnp.int32).astype(F32) * level_in[0:1]
    patch = mine + moved_left(row_pick, beside(theirs))
    obj_r, obj_i = patch[:, :width], patch[:, width:]

    wave_copy = remote(wave_out, wave, 3, (1, tile))
    back_copy = remote(back_out, back, 4, (0, tile))

    def keep_grads(psi_r, psi_i, h_r, h_i):
        grad_r, grad_i = conj_times(psi_r, psi_i, h_r, h_i)
        grads[:, :width] = grad_r
        grads[:, width:] = grad_i

    @pl.when(cut == 0)
    def first():
        chi_r, chi_i = times(illum[0], illum[1], obj_r, obj_i)
        value = from_left(jnp.concatenate([chi_r, chi_i], axis=0), mats, 2)
        value = from_right(beside(value), mats, 0)
        wave_out[...] = value.astype(BF16)
        wave_copy.start()
        wave_copy.wait_send()
        back_copy.wait_recv()
        grad = back[...]
        value = dot(grad, mats[2]) + dot(grad, mats[3])
        value = from_left(above(value), mats, 0)
        keep_grads(illum[0], illum[1], value[:width], value[width:])

    @pl.when(cut == 1)
    def second():
        wave_copy.wait_recv()
        psi = wave[...].astype(F32)
        psi_r, psi_i = psi[:, :width], psi[:, width:]
        chi_r, chi_i = times(psi_r, psi_i, obj_r, obj_i)
        value = from_right(jnp.concatenate([chi_r, chi_i], axis=1), mats, 0)
        value = from_left(above(value), mats, 2)
        out_r, out_i = value[:width], value[width:]
        weight = (out_r * out_r + out_i * out_i - measured[0]) * flag
        value = jnp.concatenate([weight * out_r, weight * out_i], axis=0)
        value = from_left(value, mats, 0)
        value = from_right(beside(value), mats, 2)
        h_r, h_i = value[:, :width], value[:, width:]
        g_r, g_i = conj_times(obj_r, obj_i, h_r, h_i)
        back_out[...] = jnp.concatenate([g_r, g_i], axis=1).astype(BF16)
        back_copy.start()
        keep_grads(psi_r, psi_i, h_r, h_i)
        back_copy.wait_send()

    total = grads[...]
    high, low = halves(total)
    spill_out[...] = dot(one_hot((rows, width), 0, row_at, rows), high).astype(BF16)
    spill = remote(spill_out, spill_in, 5, (cut, after))
    spill.start()
    row_put = one_hot((rows, width), 0, row_at)
    kept = above(dot(row_put, high) + dot(row_put, low))
    kept = moved_right(kept, one_hot((width, cols), 1, col_at))
    put = one_hot((width, cols), 1, off_in[0:1, 0:1])
    spill.wait()
    for part in range(2):
        arrived = dot(spill_in[:, part * width : (part + 1) * width], put)
        out[part] = kept[part * rows : (part + 1) * rows] + arrived


def on_device(tiles, tables, transmission, illumination, measured, offsets, live_count):
    width = illumination.shape[-1]
    trans = transmission[:, 0]
    rows, cols = trans.shape[1:]
    hbm = pl.BlockSpec(memory_space=pltpu.HBM)
    total = pl.pallas_call(
        functools.partial(kernel, tiles),
        out_shape=jax.ShapeDtypeStruct(trans.shape, F32),
        in_specs=[hbm] * 6,
        out_specs=pl.BlockSpec(memory_space=pltpu.VMEM),
        scratch_shapes=[
            pltpu.VMEM(trans.shape, F32),
            pltpu.VMEM(illumination.shape, F32),
            pltpu.VMEM(measured.shape, F32),
            pltpu.VMEM((1, 2), jnp.int32),
            pltpu.VMEM((1, 1), jnp.int32),
            pltpu.VMEM((4, 2 * width, 2 * width), BF16),
            pltpu.VMEM((8, 128), jnp.int32),
            pltpu.VMEM((8, 128), jnp.int32),
            pltpu.VMEM((2 * rows, width), jnp.int16),
            pltpu.VMEM((2 * rows, width), jnp.int16),
            pltpu.VMEM((8, width), F32),
            pltpu.VMEM((8, width), F32),
            pltpu.VMEM((width, 2 * width), BF16),
            pltpu.VMEM((width, 2 * width), BF16),
            pltpu.VMEM((width, 2 * width), BF16),
            pltpu.VMEM((width, 2 * width), BF16),
            pltpu.VMEM((width, 2 * width), F32),
            pltpu.VMEM((rows, 2 * width), BF16),
            pltpu.VMEM((rows, 2 * width), BF16),
            pltpu.SemaphoreType.DMA((6,)),
            pltpu.SemaphoreType.DMA((6,)),
            pltpu.SemaphoreType.DMA((6,)),
        ],
        compiler_params=pltpu.CompilerParams(
            collective_id=0, has_side_effects=True, vmem_limit_bytes=48 * 1024 * 1024
        ),
    )(trans, illumination, measured, offsets, live_count[:, None], jnp.asarray(tables))
    return total[:, None]


def solution(mesh):
    placed = (P(None, "cuts", "tile", None), P(), P("tile", None, None), P("tile", None), P("tile"))
    tiles = mesh.shape["tile"]

    def whole(transmission, illumination, measured, offsets, live_count):
        tables = constant_tables(illumination.shape[-1])
        return jax.shard_map(
            functools.partial(on_device, tiles, tables),
            mesh=mesh,
            in_specs=placed,
            out_specs=P(None, "cuts", "tile", None),
            check_vma=False,
        )(transmission, illumination, measured, offsets, live_count)

    return whole
```

```python
import functools
import math

import jax
import jax.numpy as jnp
import ml_dtypes
import numpy as np
from jax import lax
from jax.experimental import pallas as pl
from jax.experimental.pallas import tpu as pltpu
from jax.sharding import PartitionSpec as P

MESH = pl.DeviceIdType.MESH
F32 = jnp.float32
BF16 = jnp.bfloat16
MIDDLE = 2.6
SCALE = 13650.0


def split_pair(value):
    high = value.astype(ml_dtypes.bfloat16)
    low = (value - high.astype(np.float64)).astype(ml_dtypes.bfloat16)
    return high, low


def constant_tables(width):
    freq = np.arange(width)
    signed = np.where(freq < width // 2, freq, freq - width).astype(np.float64)
    phases = math.pi * signed * signed / (4.0 * width)
    waves = np.exp(2j * math.pi * (freq[:, None] * freq[None, :] % width) / width)
    prop = (waves * np.exp(-1j * phases)[None, :]) @ waves.conj().T / width
    far = waves.conj() / math.sqrt(width)
    rows = []
    for mat in (prop, far):
        right = np.block([[mat.real, mat.imag], [-mat.imag, mat.real]])
        left = np.block([[mat.real, -mat.imag], [mat.imag, mat.real]])
        rows.append(np.stack(split_pair(right) + split_pair(left)))
    return np.stack(rows)


def halves(value):
    high = value.astype(BF16)
    low = (value - high.astype(F32)).astype(BF16)
    return high, low


def dot(a, b):
    return jnp.dot(a, b, preferred_element_type=F32)


def from_right(value, mats, at):
    high, low = halves(value)
    return dot(high, mats[at]) + (dot(low, mats[at]) + dot(high, mats[at + 1]))


def from_left(value, mats, at):
    high, low = halves(value)
    return dot(mats[at], high) + (dot(mats[at], low) + dot(mats[at + 1], high))


def beside(stacked):
    width = stacked.shape[0] // 2
    return jnp.concatenate([stacked[:width], stacked[width:]], axis=1)


def above(flat):
    width = flat.shape[1] // 2
    return jnp.concatenate([flat[:, :width], flat[:, width:]], axis=0)


def times(ar, ai, br, bi):
    return ar * br - ai * bi, ar * bi + ai * br


def conj_times(ar, ai, br, bi):
    return ar * br + ai * bi, ar * bi - ai * br


def one_hot(shape, along, offset, start=0):
    ahead = lax.broadcasted_iota(jnp.int32, shape, along) + start
    gap = ahead - lax.broadcasted_iota(jnp.int32, shape, 1 - along)
    return jnp.where(gap == offset, 1.0, 0.0).astype(BF16)


def moved_right(value, mask):
    high, low = halves(value)
    return dot(high, mask) + dot(low, mask)


def moved_left(mask, value):
    high, low = halves(value)
    return dot(mask, high) + dot(mask, low)


def kernel(
    tiles,
    trans_hbm,
    illum_hbm,
    measured_hbm,
    offs_hbm,
    live_hbm,
    tables,
    out,
    trans,
    illum,
    measured,
    offs,
    live,
    mats,
    off_out,
    off_in,
    code_out,
    code_in,
    level_out,
    level_in,
    wave,
    back,
    wave_out,
    back_out,
    grads,
    spill_out,
    spill_in,
    target_out,
    target_in,
    turn_sem,
    local_sem,
    send_sem,
    recv_sem,
):
    cut = lax.axis_index("cuts")
    tile = lax.axis_index("tile")
    before = lax.rem(tile + tiles - 1, tiles)
    after = lax.rem(tile + 1, tiles)
    other = 1 - cut
    rows, cols = trans.shape[1], trans.shape[2]
    width = illum.shape[1]

    barrier = pltpu.get_barrier_semaphore()
    for target in ((cut, before), (other, tile)):
        pl.semaphore_signal(barrier, inc=1, device_id=target, device_id_type=MESH)
    local = []
    for source, target in (
        (offs_hbm, offs),
        (live_hbm, live),
        (trans_hbm, trans),
        (illum_hbm, illum),
        (measured_hbm, measured),
        (tables.at[cut], mats),
    ):
        copy = pltpu.make_async_copy(source, target, local_sem.at[len(local)])
        copy.start()
        local.append(copy)
    local[0].wait()
    local[1].wait()
    row_at = offs[0:1, 0:1]
    col_at = offs[0:1, 1:2]
    line = lax.broadcasted_iota(jnp.int32, off_out.shape, 0)
    off_out[...] = jnp.where(line == 0, row_at, jnp.where(line == 1, col_at, live[0:1, 0:1]))
    local[2].wait()
    pick = one_hot((cols, width), 0, col_at)
    picked = moved_right(jnp.concatenate([trans[0], trans[1]], axis=0), pick)
    level = jnp.maximum(jnp.max(jnp.abs(picked), axis=0, keepdims=True), 1e-30) * (1.0 / 32767.0)
    level_out[...] = jnp.broadcast_to(level, level_out.shape)
    code_out[...] = jnp.round(picked / level).astype(jnp.int32).astype(jnp.int16)
    pl.semaphore_wait(barrier, 2)

    def remote(src, dst, at, target):
        return pltpu.make_async_remote_copy(
            src_ref=src,
            dst_ref=dst,
            send_sem=send_sem.at[at],
            recv_sem=recv_sem.at[at],
            device_id=target,
            device_id_type=MESH,
        )

    off_copy = remote(off_out, off_in, 0, (cut, after))
    off_copy.start()
    level_copy = remote(level_out, level_in, 1, (cut, after))
    level_copy.start()
    code_copy = remote(code_out, code_in, 2, (cut, after))
    target_copy = remote(target_out, target_in, 6, (1, after))

    @pl.when(cut == 0)
    def send_first():
        code_copy.start()
        code_copy.wait_send()
        pl.semaphore_signal(turn_sem, inc=1, device_id=(other, tile), device_id_type=MESH)

    @pl.when(cut == 1)
    def send_second():
        local[4].wait()
        target_out[...] = jnp.round((measured[0] - MIDDLE) * SCALE).astype(jnp.int32).astype(jnp.int16)
        pl.semaphore_wait(turn_sem, 1)
        code_copy.start()
        target_copy.start()
        code_copy.wait_send()

    @pl.when(cut == 0)
    def rest():
        local[4].wait()

    off_copy.wait()
    their_row = off_in[0:1, 0:1]
    their_col = off_in[1:2, 0:1]
    flag = jnp.where(off_in[2:3, 0:1] > 0, 1.0, 0.0)
    pick = one_hot((cols, width), 0, their_col)
    mine = beside(moved_right(jnp.concatenate([trans[0], trans[1]], axis=0), pick))
    mine = moved_left(one_hot((width, rows), 1, their_row, rows), mine)
    row_pick = one_hot((width, rows), 1, their_row)
    local[3].wait()
    local[5].wait()
    level_copy.wait()
    code_copy.wait_recv()
    theirs = code_in[...].astype(jnp.int32).astype(F32) * level_in[0:1]
    patch = mine + moved_left(row_pick, beside(theirs))
    obj_r, obj_i = patch[:, :width], patch[:, width:]

    wave_copy = remote(wave_out, wave, 3, (1, tile))
    back_copy = remote(back_out, back, 4, (0, tile))

    def keep_grads(psi_r, psi_i, h_r, h_i):
        grad_r, grad_i = conj_times(psi_r, psi_i, h_r, h_i)
        grads[:, :width] = grad_r
        grads[:, width:] = grad_i

    @pl.when(cut == 0)
    def first():
        chi_r, chi_i = times(illum[0], illum[1], obj_r, obj_i)
        value = from_left(jnp.concatenate([chi_r, chi_i], axis=0), mats, 2)
        value = from_right(beside(value), mats, 0)
        wave_out[...] = value.astype(BF16)
        wave_copy.start()
        wave_copy.wait_send()
        back_copy.wait_recv()
        grad = back[...]
        value = dot(grad, mats[2]) + dot(grad, mats[3])
        value = from_left(above(value), mats, 0)
        keep_grads(illum[0], illum[1], value[:width], value[width:])

    @pl.when(cut == 1)
    def second():
        wave_copy.wait_recv()
        psi = wave[...].astype(F32)
        psi_r, psi_i = psi[:, :width], psi[:, width:]
        chi_r, chi_i = times(psi_r, psi_i, obj_r, obj_i)
        value = from_right(jnp.concatenate([chi_r, chi_i], axis=1), mats, 0)
        value = from_left(above(value), mats, 2)
        out_r, out_i = value[:width], value[width:]
        target_copy.wait()
        target = target_in[...].astype(jnp.int32).astype(F32) * (1.0 / SCALE) + MIDDLE
        weight = (out_r * out_r + out_i * out_i - target) * flag
        value = jnp.concatenate([weight * out_r, weight * out_i], axis=0)
        value = from_left(value, mats, 0)
        value = from_right(beside(value), mats, 2)
        h_r, h_i = value[:, :width], value[:, width:]
        g_r, g_i = conj_times(obj_r, obj_i, h_r, h_i)
        back_out[...] = jnp.concatenate([g_r, g_i], axis=1).astype(BF16)
        back_copy.start()
        keep_grads(psi_r, psi_i, h_r, h_i)
        back_copy.wait_send()

    total = grads[...]
    high, low = halves(total)
    spill_out[...] = dot(one_hot((rows, width), 0, their_row), high).astype(BF16)
    spill = remote(spill_out, spill_in, 5, (cut, before))
    spill.start()
    row_put = one_hot((rows, width), 0, their_row, rows)
    kept = above(dot(row_put, high) + dot(row_put, low))
    kept = moved_right(kept, one_hot((width, cols), 1, their_col))
    put = one_hot((width, cols), 1, col_at)
    spill.wait()
    for part in range(2):
        arrived = dot(spill_in[:, part * width : (part + 1) * width], put)
        out[part] = kept[part * rows : (part + 1) * rows] + arrived


def on_device(tiles, tables, transmission, illumination, measured, offsets, live_count):
    width = illumination.shape[-1]
    trans = transmission[:, 0]
    rows, cols = trans.shape[1:]
    hbm = pl.BlockSpec(memory_space=pltpu.HBM)
    total = pl.pallas_call(
        functools.partial(kernel, tiles),
        out_shape=jax.ShapeDtypeStruct(trans.shape, F32),
        in_specs=[hbm] * 6,
        out_specs=pl.BlockSpec(memory_space=pltpu.VMEM),
        scratch_shapes=[
            pltpu.VMEM(trans.shape, F32),
            pltpu.VMEM(illumination.shape, F32),
            pltpu.VMEM(measured.shape, F32),
            pltpu.VMEM((1, 2), jnp.int32),
            pltpu.VMEM((1, 1), jnp.int32),
            pltpu.VMEM((4, 2 * width, 2 * width), BF16),
            pltpu.VMEM((8, 128), jnp.int32),
            pltpu.VMEM((8, 128), jnp.int32),
            pltpu.VMEM((2 * rows, width), jnp.int16),
            pltpu.VMEM((2 * rows, width), jnp.int16),
            pltpu.VMEM((8, width), F32),
            pltpu.VMEM((8, width), F32),
            pltpu.VMEM((width, 2 * width), BF16),
            pltpu.VMEM((width, 2 * width), BF16),
            pltpu.VMEM((width, 2 * width), BF16),
            pltpu.VMEM((width, 2 * width), BF16),
            pltpu.VMEM((width, 2 * width), F32),
            pltpu.VMEM((rows, 2 * width), BF16),
            pltpu.VMEM((rows, 2 * width), BF16),
            pltpu.VMEM((width, width), jnp.int16),
            pltpu.VMEM((width, width), jnp.int16),
            pltpu.SemaphoreType.REGULAR,
            pltpu.SemaphoreType.DMA((6,)),
            pltpu.SemaphoreType.DMA((7,)),
            pltpu.SemaphoreType.DMA((7,)),
        ],
        compiler_params=pltpu.CompilerParams(
            collective_id=0, has_side_effects=True, vmem_limit_bytes=60 * 1024 * 1024
        ),
    )(trans, illumination, measured, offsets, live_count[:, None], jnp.asarray(tables))
    return total[:, None]


def solution(mesh):
    placed = (P(None, "cuts", "tile", None), P(), P("tile", None, None), P("tile", None), P("tile"))
    tiles = mesh.shape["tile"]

    def whole(transmission, illumination, measured, offsets, live_count):
        tables = constant_tables(illumination.shape[-1])
        return jax.shard_map(
            functools.partial(on_device, tiles, tables),
            mesh=mesh,
            in_specs=placed,
            out_specs=P(None, "cuts", "tile", None),
            check_vma=False,
        )(transmission, illumination, measured, offsets, live_count)

    return whole
```

```python
import functools
import math

import jax
import jax.numpy as jnp
import ml_dtypes
import numpy as np
from jax import lax
from jax.experimental import pallas as pl
from jax.experimental.pallas import tpu as pltpu
from jax.sharding import PartitionSpec as P

MESH = pl.DeviceIdType.MESH
F32 = jnp.float32
BF16 = jnp.bfloat16
MIDDLE = 2.6
SCALE = 13650.0
PARTS = 2


def split_pair(value):
    high = value.astype(ml_dtypes.bfloat16)
    low = (value - high.astype(np.float64)).astype(ml_dtypes.bfloat16)
    return high, low


def constant_tables(width):
    freq = np.arange(width)
    signed = np.where(freq < width // 2, freq, freq - width).astype(np.float64)
    phases = math.pi * signed * signed / (4.0 * width)
    waves = np.exp(2j * math.pi * (freq[:, None] * freq[None, :] % width) / width)
    prop = (waves * np.exp(-1j * phases)[None, :]) @ waves.conj().T / width
    far = waves.conj() / math.sqrt(width)
    rows = []
    for mat in (prop, far):
        right = np.block([[mat.real, mat.imag], [-mat.imag, mat.real]])
        left = np.block([[mat.real, -mat.imag], [mat.imag, mat.real]])
        rows.append(np.stack(split_pair(right) + split_pair(left)))
    return np.stack(rows)


def halves(value):
    high = value.astype(BF16)
    low = (value - high.astype(F32)).astype(BF16)
    return high, low


def dot(a, b):
    return jnp.dot(a, b, preferred_element_type=F32)


def from_right(value, mats, at):
    high, low = halves(value)
    count = value.shape[0]
    both = dot(jnp.concatenate([high, low], axis=0), mats[at])
    return both[:count] + (both[count:] + dot(high, mats[at + 1]))


def from_left(value, mats, at):
    high, low = halves(value)
    return dot(mats[at], high) + (dot(mats[at], low) + dot(mats[at + 1], high))


def beside(stacked):
    width = stacked.shape[0] // 2
    return jnp.concatenate([stacked[:width], stacked[width:]], axis=1)


def above(flat):
    width = flat.shape[1] // 2
    return jnp.concatenate([flat[:, :width], flat[:, width:]], axis=0)


def times(ar, ai, br, bi):
    return ar * br - ai * bi, ar * bi + ai * br


def conj_times(ar, ai, br, bi):
    return ar * br + ai * bi, ar * bi - ai * br


def one_hot(shape, along, offset, start=0):
    ahead = lax.broadcasted_iota(jnp.int32, shape, along) + start
    gap = ahead - lax.broadcasted_iota(jnp.int32, shape, 1 - along)
    return jnp.where(gap == offset, 1.0, 0.0).astype(BF16)


def moved_right(value, mask):
    high, low = halves(value)
    return dot(high, mask) + dot(low, mask)


def moved_left(mask, value):
    high, low = halves(value)
    return dot(mask, high) + dot(mask, low)


def kernel(
    tiles,
    trans_hbm,
    illum_hbm,
    measured_hbm,
    offs_hbm,
    live_hbm,
    tables,
    out,
    trans,
    illum,
    measured,
    offs,
    live,
    mats,
    off_out,
    off_in,
    code_out,
    code_in,
    level_out,
    level_in,
    wave,
    back,
    wave_out,
    back_out,
    grads,
    spill_out,
    spill_in,
    target_out,
    target_in,
    turn_sem,
    local_sem,
    send_sem,
    recv_sem,
):
    cut = lax.axis_index("cuts")
    tile = lax.axis_index("tile")
    before = lax.rem(tile + tiles - 1, tiles)
    after = lax.rem(tile + 1, tiles)
    other = 1 - cut
    rows, cols = trans.shape[1], trans.shape[2]
    width = illum.shape[1]

    barrier = pltpu.get_barrier_semaphore()
    for target in ((cut, before), (other, tile)):
        pl.semaphore_signal(barrier, inc=1, device_id=target, device_id_type=MESH)
    local = []
    for source, target in (
        (offs_hbm, offs),
        (live_hbm, live),
        (trans_hbm, trans),
        (illum_hbm, illum),
        (measured_hbm, measured),
        (tables.at[cut], mats),
    ):
        copy = pltpu.make_async_copy(source, target, local_sem.at[len(local)])
        if len(local) < 3:
            copy.start()
        local.append(copy)
    local[0].wait()
    local[1].wait()
    row_at = offs[0:1, 0:1]
    col_at = offs[0:1, 1:2]
    line = lax.broadcasted_iota(jnp.int32, off_out.shape, 0)
    off_out[...] = jnp.where(line == 0, row_at, jnp.where(line == 1, col_at, live[0:1, 0:1]))
    pick = one_hot((cols, width), 0, col_at)

    def remote(src, dst, at, target):
        return pltpu.make_async_remote_copy(
            src_ref=src,
            dst_ref=dst,
            send_sem=send_sem.at[at],
            recv_sem=recv_sem.at[at],
            device_id=target,
            device_id_type=MESH,
        )

    def per_part(src, dst, first, target):
        return [remote(src.at[c], dst.at[c], first + c, target) for c in range(PARTS)]

    off_copy = remote(off_out, off_in, 0, (cut, after))
    target_copy = remote(target_out, target_in, 1, (1, after))
    level_copies = per_part(level_out, level_in, 2, (cut, after))
    code_copies = per_part(code_out, code_in, 2 + PARTS, (cut, after))
    wave_copies = per_part(wave_out, wave, 2 + 2 * PARTS, (1, tile))
    back_copies = per_part(back_out, back, 2 + 3 * PARTS, (0, tile))
    spill_copies = per_part(spill_out, spill_in, 2 + 4 * PARTS, (cut, before))

    local[2].wait()
    for copy in local[3:]:
        copy.start()
    strip = rows // PARTS
    for c in range(PARTS):
        part = slice(c * strip, (c + 1) * strip)
        picked = moved_right(jnp.concatenate([trans[0, part], trans[1, part]], axis=0), pick)
        peak = jnp.maximum(jnp.max(jnp.abs(picked), axis=0, keepdims=True), 1e-30)
        level_out[c] = jnp.broadcast_to(peak * (1.0 / 32766.0), level_out.shape[1:])
        code = jnp.round(picked * (32766.0 / peak))
        code_out[c] = code.astype(jnp.int32).astype(jnp.int16)
        if c == 0:
            pl.semaphore_wait(barrier, 2)
            off_copy.start()
        level_copies[c].start()

        @pl.when(cut == 0)
        def send_first():
            code_copies[c].start()

    @pl.when(cut == 1)
    def code_target():
        local[4].wait()
        moved = jnp.round((measured[0] - MIDDLE) * SCALE)
        target_out[...] = moved.astype(jnp.int32).astype(jnp.int16)

    off_copy.wait()
    their_row = off_in[0:1, 0:1]
    their_col = off_in[1:2, 0:1]
    flag = jnp.where(off_in[2:3, 0:1] > 0, 1.0, 0.0)
    pick = one_hot((cols, width), 0, their_col)
    mine = beside(moved_right(jnp.concatenate([trans[0], trans[1]], axis=0), pick))
    patch = moved_left(one_hot((width, rows), 1, their_row, rows), mine)
    row_pick = one_hot((width, rows), 1, their_row)
    local[3].wait()
    local[5].wait()

    @pl.when(cut == 0)
    def pass_turn():
        for copy in code_copies:
            copy.wait_send()
        pl.semaphore_signal(turn_sem, inc=1, device_id=(other, tile), device_id_type=MESH)
        local[4].wait()

    @pl.when(cut == 1)
    def take_turn():
        pl.semaphore_wait(turn_sem, 1)
        for copy in code_copies:
            copy.start()
        target_copy.start()

    for c in range(PARTS):
        level_copies[c].wait()
        code_copies[c].wait_recv()
        theirs = code_in[c].astype(jnp.int32).astype(F32) * level_in[c, 0:1]
        patch = patch + moved_left(row_pick[:, c * strip : (c + 1) * strip], beside(theirs))
    obj_r, obj_i = patch[:, :width], patch[:, width:]
    step = width // PARTS
    parts = [slice(c * step, (c + 1) * step) for c in range(PARTS)]

    def keep_grads(c, psi_r, psi_i, h_r, h_i):
        grad = jnp.concatenate(conj_times(psi_r, psi_i, h_r, h_i), axis=1)
        grads[parts[c]] = grad
        spill_out[c] = grad.astype(BF16)
        spill_copies[c].start()

    @pl.when(cut == 0)
    def first():
        chi_r, chi_i = times(illum[0], illum[1], obj_r, obj_i)
        value = beside(from_left(jnp.concatenate([chi_r, chi_i], axis=0), mats, 2))
        for c in range(PARTS):
            wave_out[c] = from_right(value[parts[c]], mats, 0).astype(BF16)
            wave_copies[c].start()
        values = []
        for c in range(PARTS):
            back_copies[c].wait_recv()
            grad = back[c]
            values.append(dot(grad, mats[2]) + dot(grad, mats[3]))
        high, low = halves(above(jnp.concatenate(values, axis=0)))
        for c in range(PARTS):
            lead = [
                jnp.concatenate([mats[at, parts[c]], mats[at, pl.ds(width + c * step, step)]], axis=0)
                for at in range(2)
            ]
            value = dot(lead[0], high) + (dot(lead[0], low) + dot(lead[1], high))
            keep_grads(c, illum[0, parts[c]], illum[1, parts[c]], value[:step], value[step:])
        for copy in wave_copies:
            copy.wait_send()

    @pl.when(cut == 1)
    def second():
        values, waves = [], []
        for c in range(PARTS):
            wave_copies[c].wait_recv()
            psi = wave[c].astype(F32)
            psi_r, psi_i = psi[:, :width], psi[:, width:]
            chi = times(psi_r, psi_i, obj_r[parts[c]], obj_i[parts[c]])
            values.append(from_right(jnp.concatenate(chi, axis=1), mats, 0))
            waves.append((psi_r, psi_i))
        value = from_left(above(jnp.concatenate(values, axis=0)), mats, 2)
        out_r, out_i = value[:width], value[width:]
        target_copy.wait()
        target = target_in[...].astype(jnp.int32).astype(F32) * (1.0 / SCALE) + MIDDLE
        weight = (out_r * out_r + out_i * out_i - target) * flag
        value = jnp.concatenate([weight * out_r, weight * out_i], axis=0)
        value = beside(from_left(value, mats, 0))
        for c in range(PARTS):
            back_wave = from_right(value[parts[c]], mats, 2)
            h_r, h_i = back_wave[:, :width], back_wave[:, width:]
            g = conj_times(obj_r[parts[c]], obj_i[parts[c]], h_r, h_i)
            back_out[c] = jnp.concatenate(g, axis=1).astype(BF16)
            back_copies[c].start()
            keep_grads(c, *waves[c], h_r, h_i)
        for copy in back_copies + code_copies:
            copy.wait_send()

    high, low = halves(grads[...])
    row_put = one_hot((rows, width), 0, their_row, rows)
    kept = above(dot(row_put, high) + dot(row_put, low))
    kept = moved_right(kept, one_hot((width, cols), 1, their_col))
    put = one_hot((width, cols), 1, col_at)
    row_take = one_hot((rows, width), 0, row_at)
    arrived = jnp.zeros((rows, 2 * width), F32)
    for c in range(PARTS):
        spill_copies[c].wait()
        arrived = arrived + dot(row_take[:, parts[c]], spill_in[c])
    arrived = dot(above(arrived).astype(BF16), put) + kept
    for part in range(2):
        out[part] = arrived[part * rows : (part + 1) * rows]


def on_device(tiles, tables, transmission, illumination, measured, offsets, live_count):
    width = illumination.shape[-1]
    trans = transmission[:, 0]
    rows, cols = trans.shape[1:]
    hbm = pl.BlockSpec(memory_space=pltpu.HBM)
    total = pl.pallas_call(
        functools.partial(kernel, tiles),
        out_shape=pltpu.VMEM(trans.shape, F32),
        in_specs=[hbm] * 6,
        out_specs=pl.BlockSpec(memory_space=pltpu.VMEM),
        scratch_shapes=[
            pltpu.VMEM(trans.shape, F32),
            pltpu.VMEM(illumination.shape, F32),
            pltpu.VMEM(measured.shape, F32),
            pltpu.VMEM((1, 2), jnp.int32),
            pltpu.VMEM((1, 1), jnp.int32),
            pltpu.VMEM((4, 2 * width, 2 * width), BF16),
            pltpu.VMEM((8, 128), jnp.int32),
            pltpu.VMEM((8, 128), jnp.int32),
            pltpu.VMEM((PARTS, 2 * rows // PARTS, width), jnp.int16),
            pltpu.VMEM((PARTS, 2 * rows // PARTS, width), jnp.int16),
            pltpu.VMEM((PARTS, 8, width), F32),
            pltpu.VMEM((PARTS, 8, width), F32),
            pltpu.VMEM((PARTS, width // PARTS, 2 * width), BF16),
            pltpu.VMEM((PARTS, width // PARTS, 2 * width), BF16),
            pltpu.VMEM((PARTS, width // PARTS, 2 * width), BF16),
            pltpu.VMEM((PARTS, width // PARTS, 2 * width), BF16),
            pltpu.VMEM((width, 2 * width), F32),
            pltpu.VMEM((PARTS, width // PARTS, 2 * width), BF16),
            pltpu.VMEM((PARTS, width // PARTS, 2 * width), BF16),
            pltpu.VMEM((width, width), jnp.int16),
            pltpu.VMEM((width, width), jnp.int16),
            pltpu.SemaphoreType.REGULAR,
            pltpu.SemaphoreType.DMA((6,)),
            pltpu.SemaphoreType.DMA((2 + 5 * PARTS,)),
            pltpu.SemaphoreType.DMA((2 + 5 * PARTS,)),
        ],
        compiler_params=pltpu.CompilerParams(
            collective_id=0, has_side_effects=True, vmem_limit_bytes=60 * 1024 * 1024
        ),
    )(trans, illumination, measured, offsets, live_count[:, None], jnp.asarray(tables))
    return total[:, None]


def solution(mesh):
    placed = (P(None, "cuts", "tile", None), P(), P("tile", None, None), P("tile", None), P("tile"))
    tiles = mesh.shape["tile"]

    def whole(transmission, illumination, measured, offsets, live_count):
        tables = constant_tables(illumination.shape[-1])
        return jax.shard_map(
            functools.partial(on_device, tiles, tables),
            mesh=mesh,
            in_specs=placed,
            out_specs=P(None, "cuts", "tile", None),
            check_vma=False,
        )(transmission, illumination, measured, offsets, live_count)

    return whole
```
